32 devices in a mesh: groups: 2 (over y), dp: 4 (over z), mx: 2 (over x), my: 2 (over core).
Axes of the slice: x: 2, y: 2, z: 4, core: 2. Of those that a mesh axis runs over, the one named last changes fastest.
Arguments:
- activations: bfloat16 [4096, 3072], P(('groups', 'dp', 'mx'), 'my'), parts along dimension 0, may hold values from -6 to 6
- ln_gain: float32 [3072], P('my'), may hold values from 0.5 to 1.5
- w_qkv: bfloat16 [3072, 24, 384], P('my', 'mx'), may hold values from -0.109375 to 0.109375
Outputs:
- context: bfloat16 [4096, 3072], P(('groups', 'dp', 'my'), 'mx'), parts along dimension 0
- h_input: float32 [6144, 3072], P(('groups', 'mx', 'my'), 'dp'), parts along dimension 0
- h_context: float32 [6144, 3072], P(('groups', 'mx'), ('dp', 'my')), parts along dimension 0
The draws below stay inside these ranges and needn't reach their ends.
There are 2 independent parts, one for each index of `groups`. The reference program is written for one: setup_inputs(seed, part) draws one part's arguments, and reference() takes and returns one part's arrays. A program takes and returns all parts, laid end to end along the dimension named above; an argument that names none is the same for every part. Nothing has to cross between parts.
All inputs are finite; a program needn't handle non-finite values.
Results may differ from the reference program's by a relative error of at most 0.017.
Values may be sent and summed in bfloat16 or wider, within the bound.
A program may use at most 128 MiB of HBM per device.

```python
import jax
import jax.numpy as jnp
from jax import lax

D = 3072
HEADS = 24
HD = 128
P_SIZE = 512
TOKENS = 2048
N_DP = 4
N_MY = 2


def levels(own_key, shape, pieces, low, high):
    level, own = 1.0, jax.random.fold_in(own_key, 6)
    for position, parts in pieces:
        steps = jnp.exp(jax.random.uniform(jax.random.fold_in(own, position), (parts,), jnp.float32, low / len(pieces), high / len(pieces)))
        level = level * jnp.repeat(steps, shape[position] // parts).reshape([-1 if axis == position else 1 for axis in range(len(shape))])
    return level


def normal_values(rng, extent, width, most, pieces=(), held_as=jnp.bfloat16):
    values = jax.random.normal(rng, extent, jnp.float32) * width
    if len(pieces) > 0:
        values = levels(rng, extent, pieces, -0.22, 0.18) * values
    return jnp.clip(values, min=-most, max=most).astype(held_as)


def setup_inputs(seed: int = 0, part: int = 0) -> dict:
    splits = jax.random.split(jax.random.key(seed), 4)
    part_keys = jax.random.split(jax.random.fold_in(splits[3], part), 4)
    return {
        "activations": normal_values(part_keys[0], (TOKENS, D), 1.0, 6.0, ((0, 8), (1, 2))),
        "ln_gain": jnp.clip(1.0 + 0.1 * jax.random.normal(splits[1], (D,), jnp.float32), 0.5, 1.5),
        "w_qkv": normal_values(splits[2], (D, HEADS, 3 * HD), D ** -0.5, 0.109375, ((0, 2), (1, 2))),
    }


EPSILON = 1e-06

def layer_norm(inputs):
    average = lax.optimization_barrier(jnp.mean(inputs, -1, keepdims=True))
    squares = lax.optimization_barrier(jnp.mean(inputs * inputs, -1, keepdims=True))
    return (inputs - average) * lax.rsqrt(squares - average * average + EPSILON)

def gram_product(left_side, right_side):
    return lax.dot_general(left_side, right_side, (((0,), (0,)), ((), ())), preferred_element_type=jnp.float32)

def reference(activations, ln_gain, w_qkv):
    normed = (layer_norm(activations.astype(jnp.float32)) * ln_gain).astype(jnp.bfloat16)
    block_width = D // N_MY
    flat_weight = w_qkv.reshape(D, HEADS * 3 * HD)
    projected = jnp.zeros((TOKENS, HEADS * 3 * HD), jnp.float32)
    for block in range(N_MY):
        partial_sum = jnp.dot(normed[:, block * block_width:(block + 1) * block_width], flat_weight[block * block_width:(block + 1) * block_width], preferred_element_type=jnp.float32)
        rounded = lax.optimization_barrier(partial_sum.astype(jnp.bfloat16))
        projected = projected + rounded.astype(jnp.float32)
    projected = projected.reshape(TOKENS, HEADS, 3 * HD)
    queries = layer_norm(projected[:, :, :HD]).astype(jnp.bfloat16)
    key_rows = layer_norm(projected[:, :, HD:2 * HD]).astype(jnp.bfloat16)
    value_rows = projected[:, :, 2 * HD:].astype(jnp.bfloat16)
    queries = queries.reshape(N_DP, P_SIZE, HEADS, HD).astype(jnp.float32)
    key_rows = key_rows.reshape(N_DP, P_SIZE, HEADS, HD).astype(jnp.float32)
    value_rows = value_rows.reshape(N_DP, P_SIZE, HEADS, HD).astype(jnp.float32)
    scores = jnp.einsum('iqhd,ikhd->ihqk', queries, key_rows) * HD ** (-0.5)
    powers = jnp.exp(scores)
    totals = lax.optimization_barrier(jnp.sum(powers, 3))
    weights = powers.astype(jnp.bfloat16).astype(jnp.float32)
    mixture = jnp.einsum('ihqk,ikhd->iqhd', weights, value_rows) / jnp.swapaxes(totals, 1, 2)[:, :, :, None]
    context = mixture.astype(jnp.bfloat16).reshape(TOKENS, HEADS * HD)
    factor = 2.0 / TOKENS
    return (context, gram_product(normed, normed) * factor, gram_product(context, context) * factor)
```

```python
import functools

import jax
import jax.numpy as jnp
from jax import lax
from jax.experimental import pallas as pl
from jax.experimental.pallas import tpu as pltpu
from jax.sharding import PartitionSpec as P

EPSILON = 1e-06
MESH = pl.DeviceIdType.MESH


def spread_2(block, axis, owner):
    block = jnp.where(lax.axis_index(axis) == owner, block, jnp.zeros_like(block))
    return lax.psum(block, axis)


def layer_norm(inputs):
    average = jnp.mean(inputs, -1, keepdims=True)
    squares = jnp.mean(inputs * inputs, -1, keepdims=True)
    return (inputs - average) * lax.rsqrt(squares - average * average + EPSILON)


def gram_product(left_side, right_side):
    return lax.dot_general(
        left_side, right_side, (((0,), (0,)), ((), ())), preferred_element_type=jnp.float32
    )


def on_device(activations, ln_gain, w_qkv):
    row_count, feature_count = activations.shape
    widened = activations.astype(jnp.float32)
    row_sums, row_squares = lax.psum((jnp.sum(widened, 1), jnp.sum(widened * widened, 1)), "my")
    width = feature_count * lax.axis_size("my")
    average = (row_sums / width)[:, None]
    spread = (row_squares / width)[:, None] - average * average
    normed = ((widened - average) * lax.rsqrt(spread + EPSILON) * ln_gain).astype(jnp.bfloat16)
    image_rows = lax.all_gather(normed, "mx", axis=0, tiled=True)
    local_heads, triple = (w_qkv.shape[1], w_qkv.shape[2])
    head_size = triple // 3
    flat_weight = w_qkv.reshape(feature_count, local_heads * triple)
    own_rows = image_rows.shape[0] // lax.axis_size("my")
    projected = (
        lax.psum_scatter(
            jnp.dot(image_rows, flat_weight, preferred_element_type=jnp.float32).astype(
                jnp.bfloat16
            ),
            "my",
            scatter_dimension=0,
            tiled=True,
        )
        .astype(jnp.float32)
        .reshape(own_rows, local_heads, triple)
    )
    queries = layer_norm(projected[:, :, :head_size]).astype(jnp.bfloat16)
    key_rows = layer_norm(projected[:, :, head_size : 2 * head_size]).astype(jnp.bfloat16)
    value_rows = projected[:, :, 2 * head_size :].astype(jnp.bfloat16)
    all_keys, all_values = (
        lax.all_gather(key_rows, "my", axis=0, tiled=True),
        lax.all_gather(value_rows, "my", axis=0, tiled=True),
    )
    scores = jnp.einsum(
        "qhd,khd->hqk", queries, all_keys, preferred_element_type=jnp.float32
    ) * head_size ** (-0.5)
    powers = jnp.exp(scores)
    totals = jnp.sum(powers, 2)
    weights = powers.astype(jnp.bfloat16)
    mixture = jnp.einsum("hqk,khd->qhd", weights, all_values, preferred_element_type=jnp.float32)
    mixture = mixture / jnp.transpose(totals)[:, :, None]
    context = mixture.astype(jnp.bfloat16).reshape(own_rows, local_heads * head_size)
    full_rows = lax.all_gather(image_rows, "my", axis=1, tiled=True)
    tile_width = full_rows.shape[1] // (lax.axis_size("mx") * lax.axis_size("my"))
    tile_index = lax.axis_index("mx") * lax.axis_size("my") + lax.axis_index("my")
    row_block = lax.dynamic_slice_in_dim(full_rows, tile_index * tile_width, tile_width, 1)
    factor = 2.0 / (full_rows.shape[0] * lax.axis_size("dp"))
    h_input = (
        lax.psum_scatter(
            gram_product(row_block, full_rows).astype(jnp.bfloat16),
            "dp",
            scatter_dimension=1,
            tiled=True,
        ).astype(jnp.float32)
        * factor
    )
    everything = lax.all_gather(context, ("dp", "my"), axis=0, tiled=True)
    block_width = everything.shape[1]
    narrow = block_width * lax.axis_size("mx") // (lax.axis_size("dp") * lax.axis_size("my"))
    flat_index = lax.axis_index("dp") * lax.axis_size("my") + lax.axis_index("my")
    offset = flat_index * narrow
    column_piece = lax.dynamic_slice_in_dim(everything, offset % block_width, narrow, 1)
    columns = spread_2(column_piece, "mx", offset // block_width)
    h_context = gram_product(everything, columns) * factor
    return (context, h_input, h_context)


class Gather:
    def __init__(self, length, place, rows, columns, total, send, receive, share, shared, local):
        self.length, (self.z, self.x, self.c) = length, place
        self.rows, self.columns, self.total = rows, columns, total
        self.send, self.receive = send, receive
        self.share, self.shared, self.local = share, shared, local
        block = 2 * self.x + self.c
        self.owner = block == self.z
        self.relay = (self.x != self.z // 2) & (self.c == self.z % 2)

    def image(self, way, step):
        return self.z - step if way == 0 else self.z + step

    def valid(self, way, step):
        return self.z >= step if way == 0 else self.z + step < self.length

    def hop(self, way, step):
        image = self.image(way, step)
        return pltpu.make_async_remote_copy(
            src_ref=self.rows.at[image],
            dst_ref=self.rows.at[image],
            send_sem=self.send.at[way, step],
            recv_sem=self.receive.at[way, step],
            device_id={"dp": self.z + 1 if way == 0 else self.z - 1},
            device_id_type=MESH,
        )

    def hops(self, way, step):
        inside = self.z < self.length - 1 if way == 0 else self.z > 0
        return inside & self.valid(way, step)

    def arrival(self, way, step):
        image = self.image(way, step)
        return pltpu.make_async_remote_copy(
            src_ref=self.rows.at[image],
            dst_ref=self.rows.at[image],
            send_sem=self.send.at[way, step],
            recv_sem=self.receive.at[way, step - 1],
            device_id={"dp": self.z - 1 if way == 0 else self.z + 1},
            device_id_type=MESH,
        )

    def sharing(self, source, image, axis):
        other = {"my": 1 - self.c} if axis == 0 else {"mx": 1 - self.x}
        return pltpu.make_async_remote_copy(
            src_ref=source.at[image],
            dst_ref=self.columns.at[image],
            send_sem=self.share.at[image, axis],
            recv_sem=self.shared.at[image],
            device_id=other,
            device_id_type=MESH,
        )

    def own(self, image):
        return pltpu.make_async_copy(
            self.rows.at[image], self.columns.at[image], self.local.at[image]
        )

    def spread(self, image):
        @pl.when(self.owner)
        def _():
            self.sharing(self.rows, image, 1).start()
            self.sharing(self.rows, image, 0).start()
            self.own(image).start()

    def begin(self):
        for way in range(2):

            @pl.when(self.hops(way, 0))
            def _():
                self.hop(way, 0).start()

        self.spread(self.z)

    def forward(self, step):
        for way in range(2):

            @pl.when(self.valid(way, step))
            def _():
                self.arrival(way, step).wait_recv()
                if step < self.length - 1:

                    @pl.when(self.hops(way, step))
                    def _():
                        self.hop(way, step).start()

                self.spread(self.image(way, step))

    def take(self, image, first):
        @pl.when(self.owner)
        def _():
            self.own(image).wait()

        @pl.when(jnp.logical_not(self.owner))
        def _():
            self.sharing(self.rows, image, 0).wait_recv()

        @pl.when(self.relay)
        def _():
            self.sharing(self.columns, image, 0).start()

        def piece(index, carry):
            part = pl.ds(pl.multiple_of(index * 256, 256), 256)
            term = lax.dot_general(
                self.rows[image, :, part],
                self.columns[image],
                (((0,), (0,)), ((), ())),
                preferred_element_type=jnp.float32,
            )
            if first:
                self.total[part, :] = term
            else:
                self.total[part, :] += term
            return carry

        lax.fori_loop(0, self.total.shape[0] // 256, piece, 0)

    def consume(self, step):
        if step == 0:
            self.take(self.z, True)
            return
        for way in range(2):

            @pl.when(self.valid(way, step))
            def _():
                self.take(self.image(way, step), False)

    def finish(self):
        for way in range(2):
            for step in range(self.length - 1):

                @pl.when(self.hops(way, step))
                def _():
                    self.hop(way, step).wait_send()

        def one(image, carry):
            @pl.when(self.owner)
            def _():
                self.sharing(self.rows, image, 1).wait_send()
                self.sharing(self.rows, image, 0).wait_send()

            @pl.when(self.relay)
            def _():
                self.sharing(self.columns, image, 0).wait_send()

            return carry

        lax.fori_loop(0, self.length, one, 0)


def kernel(
    length, factor, head_size,
    image_ref, weight_ref, context_ref, input_ref, gram_ref,
    weights, leaving, kept, arrived,
    input_rows, input_columns, context_rows, context_columns, total,
    weight_sem, plane_sem, part_send, part_receive,
    line_send, line_receive, share_send, share_receive, local_sem, swap_sem,
):
    z, x, c = lax.axis_index("dp"), lax.axis_index("mx"), lax.axis_index("my")
    heads, _, triple = weights.shape
    half = heads // 2
    tokens, block = input_rows.shape[1:]

    def weight_copy(position):
        head = lax.rem(position + (1 - c) * half, heads)
        columns = pl.ds(pl.multiple_of(head * triple, triple), triple)
        return pltpu.make_async_copy(
            weight_ref.at[:, columns], weights.at[position], weight_sem.at[position]
        )

    def start_weight(position, carry):
        weight_copy(position).start()
        return carry

    lax.fori_loop(0, heads, start_weight, 0)

    barrier = pltpu.get_barrier_semaphore()
    pl.semaphore_signal(barrier, inc=1, device_id={"my": 1 - c}, device_id_type=MESH)
    pl.semaphore_signal(barrier, inc=1, device_id={"mx": 1 - x}, device_id_type=MESH)

    @pl.when(z > 0)
    def _():
        pl.semaphore_signal(barrier, inc=1, device_id={"dp": z - 1}, device_id_type=MESH)

    @pl.when(z < length - 1)
    def _():
        pl.semaphore_signal(barrier, inc=1, device_id={"dp": z + 1}, device_id_type=MESH)

    edges = jnp.where(z > 0, 1, 0) + jnp.where(z < length - 1, 1, 0)
    pl.semaphore_wait(barrier, 2 + edges)

    inputs = Gather(
        length, (z, x, c), input_rows, input_columns, input_ref,
        line_send.at[0], line_receive.at[0], share_send.at[0], share_receive.at[0], local_sem.at[0],
    )
    contexts = Gather(
        length, (z, x, c), context_rows, context_columns, total,
        line_send.at[1], line_receive.at[1], share_send.at[1], share_receive.at[1], local_sem.at[1],
    )

    def plane_copy():
        return pltpu.make_async_remote_copy(
            src_ref=image_ref.at[:, pl.ds(pl.multiple_of((1 - c) * block, block), block)],
            dst_ref=input_rows.at[z],
            send_sem=plane_sem.at[0],
            recv_sem=plane_sem.at[1],
            device_id={"my": 1 - c},
            device_id_type=MESH,
        )

    @pl.when(c == x)
    def _():
        plane_copy().start()
        mine = pl.ds(pl.multiple_of(c * block, block), block)
        keep = pltpu.make_async_copy(image_ref.at[:, mine], input_rows.at[z], plane_sem.at[2])
        keep.start()
        keep.wait()

    @pl.when(c != x)
    def _():
        plane_copy().wait_recv()

    inputs.begin()

    def part_copy(index):
        return pltpu.make_async_remote_copy(
            src_ref=leaving.at[index],
            dst_ref=arrived.at[index],
            send_sem=part_send.at[index],
            recv_sem=part_receive.at[index],
            device_id={"my": 1 - c},
            device_id_type=MESH,
        )

    def project_away(index, carry):
        weight_copy(index).wait()
        leaving[index] = jnp.dot(
            image_ref[...], weights[index], preferred_element_type=jnp.float32
        ).astype(jnp.bfloat16)
        part_copy(index).start()
        return carry

    lax.fori_loop(0, half, project_away, 0)

    def project_here(index, carry):
        weight_copy(half + index).wait()
        kept[index] = jnp.dot(
            image_ref[...], weights[half + index], preferred_element_type=jnp.float32
        ).astype(jnp.bfloat16)
        return carry

    lax.fori_loop(0, half, project_here, 0)

    inputs.forward(1)

    def norm(values):
        average = jnp.mean(values, -1, keepdims=True)
        squares = jnp.mean(values * values, -1, keepdims=True)
        return ((values - average) * lax.rsqrt(squares - average * average + EPSILON)).astype(
            jnp.bfloat16
        )

    def attend(index, carry):
        part_copy(index).wait_recv()
        projected = kept[index].astype(jnp.float32) + arrived[index].astype(jnp.float32)
        queries = norm(projected[:, :head_size])
        keys = norm(projected[:, head_size : 2 * head_size])
        values = projected[:, 2 * head_size :].astype(jnp.bfloat16)
        scores = lax.dot_general(
            queries, keys, (((1,), (1,)), ((), ())), preferred_element_type=jnp.float32
        ) * head_size ** (-0.5)
        powers = jnp.exp(scores)
        totals = jnp.sum(powers, 1, keepdims=True)
        mixture = jnp.dot(
            powers.astype(jnp.bfloat16), values, preferred_element_type=jnp.float32
        )
        place = pl.ds(pl.multiple_of(index * head_size, head_size), head_size)
        context_rows[z, :, place] = (mixture / totals).astype(jnp.bfloat16)
        return carry

    lax.fori_loop(0, half, attend, 0)
    contexts.begin()

    own_tokens = tokens // 2
    place = pl.ds(pl.multiple_of(c * block, block), block)

    def context_copy():
        away = pl.ds(pl.multiple_of((1 - c) * own_tokens, own_tokens), own_tokens)
        return pltpu.make_async_remote_copy(
            src_ref=context_rows.at[z, away],
            dst_ref=context_ref.at[:, place],
            send_sem=swap_sem.at[0],
            recv_sem=swap_sem.at[1],
            device_id={"my": 1 - c},
            device_id_type=MESH,
        )

    context_copy().start()
    here = pl.ds(pl.multiple_of(c * own_tokens, own_tokens), own_tokens)
    context_keep = pltpu.make_async_copy(
        context_rows.at[z, here], context_ref.at[:, place], swap_sem.at[2]
    )
    context_keep.start()

    inputs.consume(0)
    inputs.forward(2)
    inputs.consume(1)
    contexts.forward(1)
    contexts.consume(0)
    for step in range(3, length):
        inputs.forward(step)
        inputs.consume(step - 1)
        contexts.forward(step - 1)
        contexts.consume(step - 2)
    inputs.consume(length - 1)
    input_ref[...] = input_ref[...] * factor
    contexts.forward(length - 1)
    contexts.consume(length - 2)
    contexts.consume(length - 1)

    narrow = block // 2
    rows = pl.ds(pl.multiple_of(c * block, block), block)
    total[...] = total[...] * factor

    def gram_copy():
        return pltpu.make_async_remote_copy(
            src_ref=total.at[:, pl.ds(pl.multiple_of((1 - c) * narrow, narrow), narrow)],
            dst_ref=gram_ref.at[rows],
            send_sem=swap_sem.at[3],
            recv_sem=swap_sem.at[4],
            device_id={"my": 1 - c},
            device_id_type=MESH,
        )

    gram_copy().start()
    gram_ref[rows, :] = total[:, pl.ds(pl.multiple_of(c * narrow, narrow), narrow)]

    @pl.when(c == x)
    def _():
        plane_copy().wait_send()

    def part_sent(index, carry):
        part_copy(index).wait_send()
        return carry

    lax.fori_loop(0, half, part_sent, 0)
    inputs.finish()
    contexts.finish()
    context_keep.wait()
    context_copy().wait()
    gram_copy().wait()


def on_device_fused(activations, ln_gain, w_qkv):
    row_count, feature_count = activations.shape
    widened = activations.astype(jnp.float32)
    row_sums, row_squares = lax.psum((jnp.sum(widened, 1), jnp.sum(widened * widened, 1)), "my")
    width = feature_count * lax.axis_size("my")
    average = (row_sums / width)[:, None]
    spread = (row_squares / width)[:, None] - average * average
    normed = ((widened - average) * lax.rsqrt(spread + EPSILON) * ln_gain).astype(jnp.bfloat16)
    image_rows = lax.all_gather(normed, "mx", axis=0, tiled=True)
    heads, triple = w_qkv.shape[1:]
    flat_weight = w_qkv.reshape(feature_count, heads * triple)
    length, tokens, block = lax.axis_size("dp"), image_rows.shape[0], feature_count // 2
    gathered = pltpu.VMEM((length, tokens, block), jnp.bfloat16)
    part = pltpu.VMEM((heads // 2, tokens, triple), jnp.bfloat16)
    dma = pltpu.SemaphoreType.DMA
    whole = pl.BlockSpec(memory_space=pltpu.VMEM)
    return pl.pallas_call(
        functools.partial(kernel, length, 2.0 / (tokens * length), triple // 3),
        out_shape=(
            jax.ShapeDtypeStruct((tokens // 2, 2 * block), jnp.bfloat16),
            jax.ShapeDtypeStruct((block, block), jnp.float32),
            jax.ShapeDtypeStruct((2 * block, block // 2), jnp.float32),
        ),
        in_specs=[whole, pl.BlockSpec(memory_space=pl.ANY)],
        out_specs=(whole, whole, whole),
        scratch_shapes=[
            pltpu.VMEM((heads, feature_count, triple), jnp.bfloat16),
            part, part, part,
            gathered, gathered, gathered, gathered,
            pltpu.VMEM((block, block), jnp.float32),
            dma((heads,)),
            dma((3,)),
            dma((heads // 2,)),
            dma((heads // 2,)),
            dma((2, 2, length)),
            dma((2, 2, length)),
            dma((2, length, 2)),
            dma((2, length)),
            dma((2, length)),
            dma((5,)),
        ],
        compiler_params=pltpu.CompilerParams(
            collective_id=0, has_side_effects=True, vmem_limit_bytes=60 * 1024 * 1024
        ),
        cost_estimate=pl.CostEstimate(
            flops=14_000_000_000, bytes_accessed=24_000_000, transcendentals=2_000_000
        ),
        name="attention_grams",
    )(image_rows, flat_weight)


def solution(mesh):
    placed = (P(("groups", "dp", "mx"), "my"), P("my"), P("my", "mx", None))
    fused = mesh.shape["mx"] == 2 and mesh.shape["my"] == 2 and mesh.shape["dp"] == 4
    return jax.shard_map(
        on_device_fused if fused else on_device,
        mesh=mesh,
        in_specs=placed,
        out_specs=(
            P(("groups", "dp", "my"), "mx"),
            P(("groups", "mx", "my"), "dp"),
            P(("groups", "mx"), ("dp", "my")),
        ),
        check_vma=False,
    )
```

```python
import functools

import jax
import jax.numpy as jnp
from jax import lax
from jax.experimental import pallas as pl
from jax.experimental.pallas import tpu as pltpu
from jax.sharding import PartitionSpec as P

EPSILON = 1e-06
MESH = pl.DeviceIdType.MESH


def spread_2(block, axis, owner):
    block = jnp.where(lax.axis_index(axis) == owner, block, jnp.zeros_like(block))
    return lax.psum(block, axis)


def layer_norm(inputs):
    average = jnp.mean(inputs, -1, keepdims=True)
    squares = jnp.mean(inputs * inputs, -1, keepdims=True)
    return (inputs - average) * lax.rsqrt(squares - average * average + EPSILON)


def gram_product(left_side, right_side):
    return lax.dot_general(
        left_side, right_side, (((0,), (0,)), ((), ())), preferred_element_type=jnp.float32
    )


def on_device(activations, ln_gain, w_qkv):
    row_count, feature_count = activations.shape
    widened = activations.astype(jnp.float32)
    row_sums, row_squares = lax.psum((jnp.sum(widened, 1), jnp.sum(widened * widened, 1)), "my")
    width = feature_count * lax.axis_size("my")
    average = (row_sums / width)[:, None]
    spread = (row_squares / width)[:, None] - average * average
    normed = ((widened - average) * lax.rsqrt(spread + EPSILON) * ln_gain).astype(jnp.bfloat16)
    image_rows = lax.all_gather(normed, "mx", axis=0, tiled=True)
    local_heads, triple = (w_qkv.shape[1], w_qkv.shape[2])
    head_size = triple // 3
    flat_weight = w_qkv.reshape(feature_count, local_heads * triple)
    own_rows = image_rows.shape[0] // lax.axis_size("my")
    projected = (
        lax.psum_scatter(
            jnp.dot(image_rows, flat_weight, preferred_element_type=jnp.float32).astype(
                jnp.bfloat16
            ),
            "my",
            scatter_dimension=0,
            tiled=True,
        )
        .astype(jnp.float32)
        .reshape(own_rows, local_heads, triple)
    )
    queries = layer_norm(projected[:, :, :head_size]).astype(jnp.bfloat16)
    key_rows = layer_norm(projected[:, :, head_size : 2 * head_size]).astype(jnp.bfloat16)
    value_rows = projected[:, :, 2 * head_size :].astype(jnp.bfloat16)
    all_keys, all_values = (
        lax.all_gather(key_rows, "my", axis=0, tiled=True),
        lax.all_gather(value_rows, "my", axis=0, tiled=True),
    )
    scores = jnp.einsum(
        "qhd,khd->hqk", queries, all_keys, preferred_element_type=jnp.float32
    ) * head_size ** (-0.5)
    powers = jnp.exp(scores)
    totals = jnp.sum(powers, 2)
    weights = powers.astype(jnp.bfloat16)
    mixture = jnp.einsum("hqk,khd->qhd", weights, all_values, preferred_element_type=jnp.float32)
    mixture = mixture / jnp.transpose(totals)[:, :, None]
    context = mixture.astype(jnp.bfloat16).reshape(own_rows, local_heads * head_size)
    full_rows = lax.all_gather(image_rows, "my", axis=1, tiled=True)
    tile_width = full_rows.shape[1] // (lax.axis_size("mx") * lax.axis_size("my"))
    tile_index = lax.axis_index("mx") * lax.axis_size("my") + lax.axis_index("my")
    row_block = lax.dynamic_slice_in_dim(full_rows, tile_index * tile_width, tile_width, 1)
    factor = 2.0 / (full_rows.shape[0] * lax.axis_size("dp"))
    h_input = (
        lax.psum_scatter(
            gram_product(row_block, full_rows).astype(jnp.bfloat16),
            "dp",
            scatter_dimension=1,
            tiled=True,
        ).astype(jnp.float32)
        * factor
    )
    everything = lax.all_gather(context, ("dp", "my"), axis=0, tiled=True)
    block_width = everything.shape[1]
    narrow = block_width * lax.axis_size("mx") // (lax.axis_size("dp") * lax.axis_size("my"))
    flat_index = lax.axis_index("dp") * lax.axis_size("my") + lax.axis_index("my")
    offset = flat_index * narrow
    column_piece = lax.dynamic_slice_in_dim(everything, offset % block_width, narrow, 1)
    columns = spread_2(column_piece, "mx", offset // block_width)
    h_context = gram_product(everything, columns) * factor
    return (context, h_input, h_context)


class Gather:
    def __init__(self, length, place, rows, columns, total, send, receive, share, shared, local):
        self.length, (self.z, self.x, self.c) = length, place
        self.rows, self.columns, self.total = rows, columns, total
        self.send, self.receive = send, receive
        self.share, self.shared, self.local = share, shared, local
        block = 2 * self.x + self.c
        self.owner = block == self.z
        self.relay = (self.x != self.z // 2) & (self.c == self.z % 2)

    def image(self, way, step):
        return self.z - step if way == 0 else self.z + step

    def valid(self, way, step):
        return self.z >= step if way == 0 else self.z + step < self.length

    def tokens(self, part):
        rows = self.rows.shape[1] // 2
        half = self.x if part == 0 else 1 - self.x
        return pl.ds(pl.multiple_of(half * rows, rows), rows)

    def hop(self, way, step, part):
        image = self.image(way, step)
        return pltpu.make_async_remote_copy(
            src_ref=self.rows.at[image, self.tokens(part)],
            dst_ref=self.rows.at[image, self.tokens(part)],
            send_sem=self.send.at[way, step, part],
            recv_sem=self.receive.at[way, step, part],
            device_id={"dp": self.z + 1 if way == 0 else self.z - 1},
            device_id_type=MESH,
        )

    def hops(self, way, step):
        inside = self.z < self.length - 1 if way == 0 else self.z > 0
        return inside & self.valid(way, step)

    def arrival(self, way, step, part):
        image = self.image(way, step)
        return pltpu.make_async_remote_copy(
            src_ref=self.rows.at[image, self.tokens(part)],
            dst_ref=self.rows.at[image, self.tokens(part)],
            send_sem=self.send.at[way, step, part],
            recv_sem=self.receive.at[way, step - 1, part],
            device_id={"dp": self.z - 1 if way == 0 else self.z + 1},
            device_id_type=MESH,
        )

    def sharing(self, source, image, axis, part):
        other = {"my": 1 - self.c} if axis == 0 else {"mx": 1 - self.x}
        return pltpu.make_async_remote_copy(
            src_ref=source.at[image, self.tokens(part)],
            dst_ref=self.columns.at[image, self.tokens(part)],
            send_sem=self.share.at[image, axis, self.part_of(part)],
            recv_sem=self.shared.at[image, self.part_of(part)],
            device_id=other,
            device_id_type=MESH,
        )

    def part_of(self, part):
        return self.x if part == 0 else 1 - self.x

    def own(self, image, part):
        return pltpu.make_async_copy(
            self.rows.at[image, self.tokens(part)],
            self.columns.at[image, self.tokens(part)],
            self.local.at[image, part],
        )

    def spread(self, image, part):
        @pl.when(self.owner)
        def _():
            self.sharing(self.rows, image, 1, part).start()
            self.sharing(self.rows, image, 0, part).start()
            self.own(image, part).start()

    def begin(self, part):
        for way in range(2):

            @pl.when(self.hops(way, 0))
            def _():
                self.hop(way, 0, part).start()

        self.spread(self.z, part)

    def forward(self, step, part):
        for way in range(2):

            @pl.when(self.valid(way, step))
            def _():
                self.arrival(way, step, part).wait_recv()
                if step < self.length - 1:

                    @pl.when(self.hops(way, step))
                    def _():
                        self.hop(way, step, part).start()

                self.spread(self.image(way, step), part)

    def follow(self, image, half):
        rows = self.rows.shape[1] // 2
        tokens = pl.ds(pl.multiple_of(half * rows, rows), rows)
        onward = pltpu.make_async_remote_copy(
            src_ref=self.columns.at[image, tokens],
            dst_ref=self.columns.at[image, tokens],
            send_sem=self.share.at[image, 0, half],
            recv_sem=self.shared.at[image, half],
            device_id={"my": 1 - self.c},
            device_id_type=MESH,
        )

        @pl.when(jnp.logical_not(self.owner))
        def _():
            onward.wait_recv()

        @pl.when(self.relay)
        def _():
            onward.start()

    def take(self, image, first):
        for order in range(2):

            @pl.when(self.owner)
            def _():
                self.own(image, order).wait()

            half = self.z // 2 if order == 0 else 1 - self.z // 2
            self.follow(image, half)

        def piece(index, carry):
            part = pl.ds(pl.multiple_of(index * 256, 256), 256)
            term = lax.dot_general(
                self.rows[image, :, part],
                self.columns[image],
                (((0,), (0,)), ((), ())),
                preferred_element_type=jnp.float32,
            )
            if first:
                self.total[part, :] = term
            else:
                self.total[part, :] += term
            return carry

        lax.fori_loop(0, self.total.shape[0] // 256, piece, 0)

    def consume(self, step):
        if step == 0:
            self.take(self.z, True)
            return
        for way in range(2):

            @pl.when(self.valid(way, step))
            def _():
                self.take(self.image(way, step), False)

    def finish(self):
        for way in range(2):
            for step in range(self.length - 1):

                @pl.when(self.hops(way, step))
                def _():
                    for part in range(2):
                        self.hop(way, step, part).wait_send()

        def one(image, carry):
            for part in range(2):

                @pl.when(self.owner)
                def _():
                    self.sharing(self.rows, image, 1, part).wait_send()
                    self.sharing(self.rows, image, 0, part).wait_send()

                @pl.when(self.relay)
                def _():
                    self.sharing(self.columns, image, 0, part).wait_send()

            return carry

        lax.fori_loop(0, self.length, one, 0)


def kernel(
    length, factor, head_size,
    normed_ref, weight_ref, context_ref, input_ref, gram_ref,
    image_ref, weights, leaving, kept, arrived,
    input_rows, input_columns, context_rows, context_columns, total,
    weight_sem, plane_sem, part_send, part_receive,
    line_send, line_receive, share_send, share_receive, local_sem, swap_sem, side_sem,
):
    z, x, c = lax.axis_index("dp"), lax.axis_index("mx"), lax.axis_index("my")
    heads, _, triple = weights.shape
    half = heads // 2
    tokens, block = input_rows.shape[1:]

    def weight_copy(position):
        head = lax.rem(position + (1 - c) * half, heads)
        return pltpu.make_async_copy(
            weight_ref.at[head], weights.at[position], weight_sem.at[position]
        )

    def start_weight(position, carry):
        weight_copy(position).start()
        return carry

    lax.fori_loop(0, heads, start_weight, 0)

    barrier = pltpu.get_barrier_semaphore()
    pl.semaphore_signal(barrier, inc=1, device_id={"my": 1 - c}, device_id_type=MESH)
    pl.semaphore_signal(barrier, inc=1, device_id={"mx": 1 - x}, device_id_type=MESH)

    @pl.when(z > 0)
    def _():
        pl.semaphore_signal(barrier, inc=1, device_id={"dp": z - 1}, device_id_type=MESH)

    @pl.when(z < length - 1)
    def _():
        pl.semaphore_signal(barrier, inc=1, device_id={"dp": z + 1}, device_id_type=MESH)

    edges = jnp.where(z > 0, 1, 0) + jnp.where(z < length - 1, 1, 0)
    pl.semaphore_wait(barrier, 2 + edges)

    inputs = Gather(
        length, (z, x, c), input_rows, input_columns, input_ref,
        line_send.at[0], line_receive.at[0], share_send.at[0], share_receive.at[0], local_sem.at[0],
    )
    contexts = Gather(
        length, (z, x, c), context_rows, context_columns, total,
        line_send.at[1], line_receive.at[1], share_send.at[1], share_receive.at[1], local_sem.at[1],
    )

    side = tokens // 2
    own_side = pl.ds(pl.multiple_of(x * side, side), side)
    far_side = pl.ds(pl.multiple_of((1 - x) * side, side), side)

    def side_copy():
        return pltpu.make_async_remote_copy(
            src_ref=normed_ref,
            dst_ref=image_ref.at[own_side],
            send_sem=side_sem.at[0],
            recv_sem=side_sem.at[1],
            device_id={"mx": 1 - x},
            device_id_type=MESH,
        )

    def plane_copy(part):
        away = pl.ds(pl.multiple_of((1 - c) * block, block), block)
        source = normed_ref.at[:, away] if part == 0 else image_ref.at[far_side, away]
        return pltpu.make_async_remote_copy(
            src_ref=source,
            dst_ref=input_rows.at[z, own_side if part == 0 else far_side],
            send_sem=plane_sem.at[0, part],
            recv_sem=plane_sem.at[1, part],
            device_id={"my": 1 - c},
            device_id_type=MESH,
        )

    def start_inputs(part):
        mine = pl.ds(pl.multiple_of(c * block, block), block)

        @pl.when(c == x)
        def _():
            if part == 1:
                side_copy().wait_recv()
            plane_copy(part).start()
            if part == 0:
                input_rows[z, own_side] = normed_ref[:, mine]
            else:
                input_rows[z, far_side] = image_ref[far_side, mine]

        @pl.when(c != x)
        def _():
            plane_copy(part).wait_recv()

        inputs.begin(part)

    @pl.when(c != x)
    def _():
        side_copy().start()

    start_inputs(0)

    def part_copy(index):
        return pltpu.make_async_remote_copy(
            src_ref=leaving.at[index],
            dst_ref=arrived.at[index],
            send_sem=part_send.at[index],
            recv_sem=part_receive.at[index],
            device_id={"my": 1 - c},
            device_id_type=MESH,
        )

    def product(rows, position):
        return jnp.dot(rows, weights[position], preferred_element_type=jnp.float32).astype(
            jnp.bfloat16
        )

    def away_near(index, carry):
        weight_copy(index).wait()
        leaving[index, own_side] = product(normed_ref[...], index)
        return carry

    def here_near(index, carry):
        weight_copy(half + index).wait()
        kept[index, own_side] = product(normed_ref[...], half + index)
        return carry

    def away_far(index, carry):
        leaving[index, far_side] = product(image_ref[far_side], index)
        part_copy(index).start()
        return carry

    def here_far(index, carry):
        kept[index, far_side] = product(image_ref[far_side], half + index)
        return carry

    lax.fori_loop(0, half, away_near, 0)

    @pl.when(c == x)
    def _():
        side_copy().start()

    lax.fori_loop(0, half, here_near, 0)
    start_inputs(1)

    @pl.when(c != x)
    def _():
        side_copy().wait_recv()

    lax.fori_loop(0, half, away_far, 0)
    inputs.forward(1, 0)
    lax.fori_loop(0, half, here_far, 0)
    inputs.forward(1, 1)

    def norm(values):
        average = jnp.mean(values, -1, keepdims=True)
        squares = jnp.mean(values * values, -1, keepdims=True)
        return ((values - average) * lax.rsqrt(squares - average * average + EPSILON)).astype(
            jnp.bfloat16
        )

    def attend(part, index, carry):
        rows = own_side if part == 0 else far_side
        if part == 0:
            part_copy(index).wait_recv()

        def projected(tokens, first, last):
            return kept[index, tokens, first:last].astype(jnp.float32) + arrived[
                index, tokens, first:last
            ].astype(jnp.float32)

        every = slice(None)
        queries = norm(projected(rows, 0, head_size))
        keys = norm(projected(every, head_size, 2 * head_size))
        values = projected(every, 2 * head_size, 3 * head_size).astype(jnp.bfloat16)
        scores = lax.dot_general(
            queries, keys, (((1,), (1,)), ((), ())), preferred_element_type=jnp.float32
        ) * head_size ** (-0.5)
        powers = jnp.exp(scores)
        totals = jnp.sum(powers, 1, keepdims=True)
        mixture = jnp.dot(
            powers.astype(jnp.bfloat16), values, preferred_element_type=jnp.float32
        )
        place = pl.ds(pl.multiple_of(index * head_size, head_size), head_size)
        context_rows[z, rows, place] = (mixture / totals).astype(jnp.bfloat16)
        return carry

    lax.fori_loop(0, half, functools.partial(attend, 0), 0)
    contexts.begin(0)
    inputs.forward(2, 0)
    lax.fori_loop(0, half, functools.partial(attend, 1), 0)
    contexts.begin(1)

    own_tokens = tokens // 2
    place = pl.ds(pl.multiple_of(c * block, block), block)

    def context_copy():
        away = pl.ds(pl.multiple_of((1 - c) * own_tokens, own_tokens), own_tokens)
        return pltpu.make_async_remote_copy(
            src_ref=context_rows.at[z, away],
            dst_ref=context_ref.at[:, place],
            send_sem=swap_sem.at[0],
            recv_sem=swap_sem.at[1],
            device_id={"my": 1 - c},
            device_id_type=MESH,
        )

    context_copy().start()
    here = pl.ds(pl.multiple_of(c * own_tokens, own_tokens), own_tokens)
    context_keep = pltpu.make_async_copy(
        context_rows.at[z, here], context_ref.at[:, place], swap_sem.at[2]
    )
    context_keep.start()

    inputs.consume(0)
    inputs.forward(2, 1)
    inputs.consume(1)
    contexts.forward(1, 0)
    contexts.forward(1, 1)
    contexts.consume(0)
    for step in range(3, length):
        inputs.forward(step, 0)
        inputs.forward(step, 1)
        inputs.consume(step - 1)
        contexts.forward(step - 1, 0)
        contexts.forward(step - 1, 1)
        contexts.consume(step - 2)
    inputs.consume(length - 1)
    input_ref[...] = input_ref[...] * factor
    contexts.forward(length - 1, 0)
    contexts.forward(length - 1, 1)
    contexts.consume(length - 2)
    contexts.consume(length - 1)

    narrow = block // 2
    rows = pl.ds(pl.multiple_of(c * block, block), block)
    total[...] = total[...] * factor

    def gram_copy():
        return pltpu.make_async_remote_copy(
            src_ref=total.at[:, pl.ds(pl.multiple_of((1 - c) * narrow, narrow), narrow)],
            dst_ref=gram_ref.at[rows],
            send_sem=swap_sem.at[3],
            recv_sem=swap_sem.at[4],
            device_id={"my": 1 - c},
            device_id_type=MESH,
        )

    gram_copy().start()
    gram_ref[rows, :] = total[:, pl.ds(pl.multiple_of(c * narrow, narrow), narrow)]

    @pl.when(c == x)
    def _():
        plane_copy(0).wait_send()
        plane_copy(1).wait_send()

    side_copy().wait_send()

    def part_sent(index, carry):
        part_copy(index).wait_send()
        return carry

    lax.fori_loop(0, half, part_sent, 0)
    inputs.finish()
    contexts.finish()
    context_keep.wait()
    context_copy().wait()
    gram_copy().wait()


def on_device_fused(activations, ln_gain, w_qkv):
    row_count, feature_count = activations.shape
    widened = activations.astype(jnp.float32)
    row_sums, row_squares = lax.psum((jnp.sum(widened, 1), jnp.sum(widened * widened, 1)), "my")
    width = feature_count * lax.axis_size("my")
    average = (row_sums / width)[:, None]
    spread = (row_squares / width)[:, None] - average * average
    normed = ((widened - average) * lax.rsqrt(spread + EPSILON) * ln_gain).astype(jnp.bfloat16)
    heads, triple = w_qkv.shape[1:]
    head_weight = jnp.transpose(w_qkv, (1, 0, 2))
    tokens = row_count * lax.axis_size("mx")
    length, block = lax.axis_size("dp"), feature_count // 2
    gathered = pltpu.VMEM((length, tokens, block), jnp.bfloat16)
    part = pltpu.VMEM((heads // 2, tokens, triple), jnp.bfloat16)
    dma = pltpu.SemaphoreType.DMA
    whole = pl.BlockSpec(memory_space=pltpu.VMEM)
    return pl.pallas_call(
        functools.partial(kernel, length, 2.0 / (tokens * length), triple // 3),
        out_shape=(
            jax.ShapeDtypeStruct((tokens // 2, 2 * block), jnp.bfloat16),
            jax.ShapeDtypeStruct((block, block), jnp.float32),
            jax.ShapeDtypeStruct((2 * block, block // 2), jnp.float32),
        ),
        in_specs=[whole, pl.BlockSpec(memory_space=pl.ANY)],
        out_specs=(whole, whole, whole),
        scratch_shapes=[
            pltpu.VMEM((tokens, feature_count), jnp.bfloat16),
            pltpu.VMEM((heads, feature_count, triple), jnp.bfloat16),
            part, part, part,
            gathered, gathered, gathered, gathered,
            pltpu.VMEM((block, block), jnp.float32),
            dma((heads,)),
            dma((2, 2)),
            dma((heads // 2,)),
            dma((heads // 2,)),
            dma((2, 2, length, 2)),
            dma((2, 2, length, 2)),
            dma((2, length, 2, 2)),
            dma((2, length, 2)),
            dma((2, length, 2)),
            dma((5,)),
            dma((2,)),
        ],
        compiler_params=pltpu.CompilerParams(
            collective_id=0, has_side_effects=True, vmem_limit_bytes=60 * 1024 * 1024
        ),
        cost_estimate=pl.CostEstimate(
            flops=14_000_000_000, bytes_accessed=24_000_000, transcendentals=2_000_000
        ),
        name="attention_grams",
    )(normed, head_weight)


def solution(mesh):
    placed = (P(("groups", "dp", "mx"), "my"), P("my"), P("my", "mx", None))
    fused = mesh.shape["mx"] == 2 and mesh.shape["my"] == 2 and mesh.shape["dp"] == 4
    return jax.shard_map(
        on_device_fused if fused else on_device,
        mesh=mesh,
        in_specs=placed,
        out_specs=(
            P(("groups", "dp", "my"), "mx"),
            P(("groups", "mx", "my"), "dp"),
            P(("groups", "mx"), ("dp", "my")),
        ),
        check_vma=False,
    )
```

```python
import functools

import jax
import jax.numpy as jnp
from jax import lax
from jax.experimental import pallas as pl
from jax.experimental.pallas import tpu as pltpu
from jax.sharding import PartitionSpec as P

EPSILON = 1e-06
MESH = pl.DeviceIdType.MESH


def spread_2(block, axis, owner):
    block = jnp.where(lax.axis_index(axis) == owner, block, jnp.zeros_like(block))
    return lax.psum(block, axis)


def layer_norm(inputs):
    average = jnp.mean(inputs, -1, keepdims=True)
    squares = jnp.mean(inputs * inputs, -1, keepdims=True)
    return (inputs - average) * lax.rsqrt(squares - average * average + EPSILON)


def gram_product(left_side, right_side):
    return lax.dot_general(
        left_side, right_side, (((0,), (0,)), ((), ())), preferred_element_type=jnp.float32
    )


def on_device(activations, ln_gain, w_qkv):
    row_count, feature_count = activations.shape
    widened = activations.astype(jnp.float32)
    row_sums, row_squares = lax.psum((jnp.sum(widened, 1), jnp.sum(widened * widened, 1)), "my")
    width = feature_count * lax.axis_size("my")
    average = (row_sums / width)[:, None]
    spread = (row_squares / width)[:, None] - average * average
    normed = ((widened - average) * lax.rsqrt(spread + EPSILON) * ln_gain).astype(jnp.bfloat16)
    image_rows = lax.all_gather(normed, "mx", axis=0, tiled=True)
    local_heads, triple = (w_qkv.shape[1], w_qkv.shape[2])
    head_size = triple // 3
    flat_weight = w_qkv.reshape(feature_count, local_heads * triple)
    own_rows = image_rows.shape[0] // lax.axis_size("my")
    projected = (
        lax.psum_scatter(
            jnp.dot(image_rows, flat_weight, preferred_element_type=jnp.float32).astype(
                jnp.bfloat16
            ),
            "my",
            scatter_dimension=0,
            tiled=True,
        )
        .astype(jnp.float32)
        .reshape(own_rows, local_heads, triple)
    )
    queries = layer_norm(projected[:, :, :head_size]).astype(jnp.bfloat16)
    key_rows = layer_norm(projected[:, :, head_size : 2 * head_size]).astype(jnp.bfloat16)
    value_rows = projected[:, :, 2 * head_size :].astype(jnp.bfloat16)
    all_keys, all_values = (
        lax.all_gather(key_rows, "my", axis=0, tiled=True),
        lax.all_gather(value_rows, "my", axis=0, tiled=True),
    )
    scores = jnp.einsum(
        "qhd,khd->hqk", queries, all_keys, preferred_element_type=jnp.float32
    ) * head_size ** (-0.5)
    powers = jnp.exp(scores)
    totals = jnp.sum(powers, 2)
    weights = powers.astype(jnp.bfloat16)
    mixture = jnp.einsum("hqk,khd->qhd", weights, all_values, preferred_element_type=jnp.float32)
    mixture = mixture / jnp.transpose(totals)[:, :, None]
    context = mixture.astype(jnp.bfloat16).reshape(own_rows, local_heads * head_size)
    full_rows = lax.all_gather(image_rows, "my", axis=1, tiled=True)
    tile_width = full_rows.shape[1] // (lax.axis_size("mx") * lax.axis_size("my"))
    tile_index = lax.axis_index("mx") * lax.axis_size("my") + lax.axis_index("my")
    row_block = lax.dynamic_slice_in_dim(full_rows, tile_index * tile_width, tile_width, 1)
    factor = 2.0 / (full_rows.shape[0] * lax.axis_size("dp"))
    h_input = (
        lax.psum_scatter(
            gram_product(row_block, full_rows).astype(jnp.bfloat16),
            "dp",
            scatter_dimension=1,
            tiled=True,
        ).astype(jnp.float32)
        * factor
    )
    everything = lax.all_gather(context, ("dp", "my"), axis=0, tiled=True)
    block_width = everything.shape[1]
    narrow = block_width * lax.axis_size("mx") // (lax.axis_size("dp") * lax.axis_size("my"))
    flat_index = lax.axis_index("dp") * lax.axis_size("my") + lax.axis_index("my")
    offset = flat_index * narrow
    column_piece = lax.dynamic_slice_in_dim(everything, offset % block_width, narrow, 1)
    columns = spread_2(column_piece, "mx", offset // block_width)
    h_context = gram_product(everything, columns) * factor
    return (context, h_input, h_context)


class Gather:
    def __init__(self, length, place, rows, columns, total, send, receive, share, shared, local):
        self.length, (self.z, self.x, self.c) = length, place
        self.rows, self.columns, self.total = rows, columns, total
        self.send, self.receive = send, receive
        self.share, self.shared, self.local = share, shared, local
        block = 2 * self.x + self.c
        self.owner = block == self.z
        self.relay = (self.x != self.z // 2) & (self.c == self.z % 2)

    def image(self, way, step):
        return self.z - step if way == 0 else self.z + step

    def valid(self, way, step):
        return self.z >= step if way == 0 else self.z + step < self.length

    def tokens(self, part):
        rows = self.rows.shape[1] // 2
        half = self.x if part == 0 else 1 - self.x
        return pl.ds(pl.multiple_of(half * rows, rows), rows)

    def hop(self, way, step, part):
        image = self.image(way, step)
        return pltpu.make_async_remote_copy(
            src_ref=self.rows.at[image, self.tokens(part)],
            dst_ref=self.rows.at[image, self.tokens(part)],
            send_sem=self.send.at[way, step, part],
            recv_sem=self.receive.at[way, step, part],
            device_id={"dp": self.z + 1 if way == 0 else self.z - 1},
            device_id_type=MESH,
        )

    def hops(self, way, step):
        inside = self.z < self.length - 1 if way == 0 else self.z > 0
        return inside & self.valid(way, step)

    def arrival(self, way, step, part):
        image = self.image(way, step)
        return pltpu.make_async_remote_copy(
            src_ref=self.rows.at[image, self.tokens(part)],
            dst_ref=self.rows.at[image, self.tokens(part)],
            send_sem=self.send.at[way, step, part],
            recv_sem=self.receive.at[way, step - 1, part],
            device_id={"dp": self.z - 1 if way == 0 else self.z + 1},
            device_id_type=MESH,
        )

    def sharing(self, source, image, axis, part):
        other = {"my": 1 - self.c} if axis == 0 else {"mx": 1 - self.x}
        return pltpu.make_async_remote_copy(
            src_ref=source.at[image, self.tokens(part)],
            dst_ref=self.columns.at[image, self.tokens(part)],
            send_sem=self.share.at[image, axis, self.part_of(part)],
            recv_sem=self.shared.at[image, self.part_of(part)],
            device_id=other,
            device_id_type=MESH,
        )

    def part_of(self, part):
        return self.x if part == 0 else 1 - self.x

    def own(self, image, part):
        return pltpu.make_async_copy(
            self.rows.at[image, self.tokens(part)],
            self.columns.at[image, self.tokens(part)],
            self.local.at[image, part],
        )

    def spread(self, image, part):
        @pl.when(self.owner)
        def _():
            self.sharing(self.rows, image, 1, part).start()
            self.sharing(self.rows, image, 0, part).start()
            self.own(image, part).start()

    def begin(self, part):
        for way in range(2):

            @pl.when(self.hops(way, 0))
            def _():
                self.hop(way, 0, part).start()

        self.spread(self.z, part)

    def forward(self, step, part):
        for way in range(2):

            @pl.when(self.valid(way, step))
            def _():
                self.arrival(way, step, part).wait_recv()
                if step < self.length - 1:

                    @pl.when(self.hops(way, step))
                    def _():
                        self.hop(way, step, part).start()

                self.spread(self.image(way, step), part)

    def follow(self, image, half):
        rows = self.rows.shape[1] // 2
        tokens = pl.ds(pl.multiple_of(half * rows, rows), rows)
        onward = pltpu.make_async_remote_copy(
            src_ref=self.columns.at[image, tokens],
            dst_ref=self.columns.at[image, tokens],
            send_sem=self.share.at[image, 0, half],
            recv_sem=self.shared.at[image, half],
            device_id={"my": 1 - self.c},
            device_id_type=MESH,
        )

        @pl.when(jnp.logical_not(self.owner))
        def _():
            onward.wait_recv()

        @pl.when(self.relay)
        def _():
            onward.start()

    def take(self, image, first):
        for order in range(2):

            @pl.when(self.owner)
            def _():
                self.own(image, order).wait()

            half = self.z // 2 if order == 0 else 1 - self.z // 2
            self.follow(image, half)

        def piece(index, carry):
            part = pl.ds(pl.multiple_of(index * 256, 256), 256)
            term = lax.dot_general(
                self.rows[image, :, part],
                self.columns[image],
                (((0,), (0,)), ((), ())),
                preferred_element_type=jnp.float32,
            )
            if first:
                self.total[part, :] = term
            else:
                self.total[part, :] += term
            return carry

        lax.fori_loop(0, self.total.shape[0] // 256, piece, 0)

    def consume(self, step):
        if step == 0:
            self.take(self.z, True)
            return
        for way in range(2):

            @pl.when(self.valid(way, step))
            def _():
                self.take(self.image(way, step), False)

    def finish(self):
        for way in range(2):
            for step in range(self.length - 1):

                @pl.when(self.hops(way, step))
                def _():
                    for part in range(2):
                        self.hop(way, step, part).wait_send()

        def one(image, carry):
            for part in range(2):

                @pl.when(self.owner)
                def _():
                    self.sharing(self.rows, image, 1, part).wait_send()
                    self.sharing(self.rows, image, 0, part).wait_send()

                @pl.when(self.relay)
                def _():
                    self.sharing(self.columns, image, 0, part).wait_send()

            return carry

        lax.fori_loop(0, self.length, one, 0)


def kernel(
    length, head_size,
    activation_ref, gain_ref, weight_ref, context_ref, input_ref, gram_ref,
    normed_ref, sums, other_sums, input_total, leaving_gram, image_ref, weights, leaving, kept, arrived,
    input_rows, input_columns, context_rows, context_columns, total,
    weight_sem, plane_sem, part_send, part_receive,
    line_send, line_receive, share_send, share_receive, local_sem, swap_sem, side_sem, sum_sem,
):
    z, x, c = lax.axis_index("dp"), lax.axis_index("mx"), lax.axis_index("my")
    heads, _, triple = weights.shape
    half = heads // 2
    tokens, block = input_rows.shape[1:]

    def weight_copy(position):
        head = lax.rem(position + (1 - c) * half, heads)
        return pltpu.make_async_copy(
            weight_ref.at[head], weights.at[position], weight_sem.at[position]
        )

    def start_weight(position, carry):
        weight_copy(position).start()
        return carry

    lax.fori_loop(0, heads, start_weight, 0)

    features = activation_ref.shape[1]
    tile = 64

    def tile_rows(index):
        return pl.ds(pl.multiple_of(index * tile, tile), tile)

    def add_up(index, carry):
        rows = tile_rows(index)
        values = activation_ref[rows, :].astype(jnp.float32)
        lanes = (tile, sums.shape[2])
        sums[0, rows] = jnp.broadcast_to(jnp.sum(values, 1, keepdims=True), lanes)
        sums[1, rows] = jnp.broadcast_to(jnp.sum(values * values, 1, keepdims=True), lanes)
        return carry

    lax.fori_loop(0, activation_ref.shape[0] // tile, add_up, 0)

    barrier = pltpu.get_barrier_semaphore()
    pl.semaphore_signal(barrier, inc=1, device_id={"my": 1 - c}, device_id_type=MESH)
    pl.semaphore_signal(barrier, inc=1, device_id={"mx": 1 - x}, device_id_type=MESH)

    @pl.when(z > 0)
    def _():
        pl.semaphore_signal(barrier, inc=1, device_id={"dp": z - 1}, device_id_type=MESH)

    @pl.when(z < length - 1)
    def _():
        pl.semaphore_signal(barrier, inc=1, device_id={"dp": z + 1}, device_id_type=MESH)

    edges = jnp.where(z > 0, 1, 0) + jnp.where(z < length - 1, 1, 0)
    pl.semaphore_wait(barrier, 2 + edges)

    def sum_copy():
        return pltpu.make_async_remote_copy(
            src_ref=sums,
            dst_ref=other_sums,
            send_sem=sum_sem.at[0],
            recv_sem=sum_sem.at[1],
            device_id={"my": 1 - c},
            device_id_type=MESH,
        )

    sum_copy().start()
    sum_copy().wait()

    def normalise(index, carry):
        rows = tile_rows(index)
        width = features * 2
        average = (sums[0, rows, 0:1] + other_sums[0, rows, 0:1]) / width
        squares = (sums[1, rows, 0:1] + other_sums[1, rows, 0:1]) / width
        values = activation_ref[rows, :].astype(jnp.float32)
        scale = lax.rsqrt(squares - average * average + EPSILON)
        normed_ref[rows, :] = ((values - average) * scale * gain_ref[...]).astype(jnp.bfloat16)
        return carry

    lax.fori_loop(0, activation_ref.shape[0] // tile, normalise, 0)

    inputs = Gather(
        length, (z, x, c), input_rows, input_columns, input_total,
        line_send.at[0], line_receive.at[0], share_send.at[0], share_receive.at[0], local_sem.at[0],
    )
    contexts = Gather(
        length, (z, x, c), context_rows, context_columns, total,
        line_send.at[1], line_receive.at[1], share_send.at[1], share_receive.at[1], local_sem.at[1],
    )

    side = tokens // 2
    own_side = pl.ds(pl.multiple_of(x * side, side), side)
    far_side = pl.ds(pl.multiple_of((1 - x) * side, side), side)

    def side_copy():
        return pltpu.make_async_remote_copy(
            src_ref=normed_ref,
            dst_ref=image_ref.at[own_side],
            send_sem=side_sem.at[0],
            recv_sem=side_sem.at[1],
            device_id={"mx": 1 - x},
            device_id_type=MESH,
        )

    def plane_copy(part):
        away = pl.ds(pl.multiple_of((1 - c) * block, block), block)
        source = normed_ref.at[:, away] if part == 0 else image_ref.at[far_side, away]
        return pltpu.make_async_remote_copy(
            src_ref=source,
            dst_ref=input_rows.at[z, own_side if part == 0 else far_side],
            send_sem=plane_sem.at[0, part],
            recv_sem=plane_sem.at[1, part],
            device_id={"my": 1 - c},
            device_id_type=MESH,
        )

    def start_inputs(part):
        mine = pl.ds(pl.multiple_of(c * block, block), block)

        @pl.when(c == x)
        def _():
            if part == 1:
                side_copy().wait_recv()
            plane_copy(part).start()
            if part == 0:
                input_rows[z, own_side] = normed_ref[:, mine]
            else:
                input_rows[z, far_side] = image_ref[far_side, mine]

        @pl.when(c != x)
        def _():
            plane_copy(part).wait_recv()

        inputs.begin(part)

    @pl.when(c != x)
    def _():
        side_copy().start()

    start_inputs(0)

    def part_copy(index):
        return pltpu.make_async_remote_copy(
            src_ref=leaving.at[index],
            dst_ref=arrived.at[index],
            send_sem=part_send.at[index],
            recv_sem=part_receive.at[index],
            device_id={"my": 1 - c},
            device_id_type=MESH,
        )

    def product(rows, position):
        return jnp.dot(rows, weights[position], preferred_element_type=jnp.float32).astype(
            jnp.bfloat16
        )

    def away_near(index, carry):
        weight_copy(index).wait()
        leaving[index, own_side] = product(normed_ref[...], index)
        return carry

    def here_near(index, carry):
        weight_copy(half + index).wait()
        kept[index, own_side] = product(normed_ref[...], half + index)
        return carry

    def away_far(index, carry):
        leaving[index, far_side] = product(image_ref[far_side], index)
        part_copy(index).start()
        return carry

    def here_far(index, carry):
        kept[index, far_side] = product(image_ref[far_side], half + index)
        return carry

    lax.fori_loop(0, half, away_near, 0)

    @pl.when(c == x)
    def _():
        side_copy().start()

    lax.fori_loop(0, half, here_near, 0)
    start_inputs(1)

    @pl.when(c != x)
    def _():
        side_copy().wait_recv()

    lax.fori_loop(0, half, away_far, 0)
    inputs.forward(1, 0)
    lax.fori_loop(0, half, here_far, 0)
    inputs.forward(1, 1)

    def norm(values):
        average = jnp.mean(values, -1, keepdims=True)
        squares = jnp.mean(values * values, -1, keepdims=True)
        return ((values - average) * lax.rsqrt(squares - average * average + EPSILON)).astype(
            jnp.bfloat16
        )

    def attend(part, index, carry):
        rows = own_side if part == 0 else far_side
        if part == 0:
            part_copy(index).wait_recv()

        def projected(tokens, first, last):
            return kept[index, tokens, first:last].astype(jnp.float32) + arrived[
                index, tokens, first:last
            ].astype(jnp.float32)

        every = slice(None)
        queries = norm(projected(rows, 0, head_size))
        keys = norm(projected(every, head_size, 2 * head_size))
        values = projected(every, 2 * head_size, 3 * head_size).astype(jnp.bfloat16)
        scores = lax.dot_general(
            queries, keys, (((1,), (1,)), ((), ())), preferred_element_type=jnp.float32
        ) * head_size ** (-0.5)
        powers = jnp.exp(scores)
        totals = jnp.sum(powers, 1, keepdims=True)
        mixture = jnp.dot(
            powers.astype(jnp.bfloat16), values, preferred_element_type=jnp.float32
        )
        place = pl.ds(pl.multiple_of(index * head_size, head_size), head_size)
        context_rows[z, rows, place] = (mixture / totals).astype(jnp.bfloat16)
        return carry

    lax.fori_loop(0, half, functools.partial(attend, 0), 0)
    contexts.begin(0)
    inputs.forward(2, 0)
    lax.fori_loop(0, half, functools.partial(attend, 1), 0)
    contexts.begin(1)

    own_tokens = tokens // 2
    place = pl.ds(pl.multiple_of(c * block, block), block)

    def context_copy():
        away = pl.ds(pl.multiple_of((1 - c) * own_tokens, own_tokens), own_tokens)
        return pltpu.make_async_remote_copy(
            src_ref=context_rows.at[z, away],
            dst_ref=context_ref.at[:, place],
            send_sem=swap_sem.at[0],
            recv_sem=swap_sem.at[1],
            device_id={"my": 1 - c},
            device_id_type=MESH,
        )

    context_copy().start()
    here = pl.ds(pl.multiple_of(c * own_tokens, own_tokens), own_tokens)
    context_keep = pltpu.make_async_copy(
        context_rows.at[z, here], context_ref.at[:, place], swap_sem.at[2]
    )
    context_keep.start()

    inputs.consume(0)
    inputs.forward(2, 1)
    inputs.consume(1)
    contexts.forward(1, 0)
    contexts.forward(1, 1)
    contexts.consume(0)
    for step in range(3, length):
        inputs.forward(step, 0)
        inputs.forward(step, 1)
        inputs.consume(step - 1)
        contexts.forward(step - 1, 0)
        contexts.forward(step - 1, 1)
        contexts.consume(step - 2)
    inputs.consume(length - 1)
    input_ref[...] = input_total[...].astype(jnp.bfloat16)
    contexts.forward(length - 1, 0)
    contexts.forward(length - 1, 1)
    contexts.consume(length - 2)
    contexts.consume(length - 1)

    narrow = block // 2
    rows = pl.ds(pl.multiple_of(c * block, block), block)
    leaving_gram[...] = total[
        :, pl.ds(pl.multiple_of((1 - c) * narrow, narrow), narrow)
    ].astype(jnp.bfloat16)

    def gram_copy():
        return pltpu.make_async_remote_copy(
            src_ref=leaving_gram,
            dst_ref=gram_ref.at[rows],
            send_sem=swap_sem.at[3],
            recv_sem=swap_sem.at[4],
            device_id={"my": 1 - c},
            device_id_type=MESH,
        )

    gram_copy().start()
    gram_ref[rows, :] = total[
        :, pl.ds(pl.multiple_of(c * narrow, narrow), narrow)
    ].astype(jnp.bfloat16)

    @pl.when(c == x)
    def _():
        plane_copy(0).wait_send()
        plane_copy(1).wait_send()

    side_copy().wait_send()

    def part_sent(index, carry):
        part_copy(index).wait_send()
        return carry

    lax.fori_loop(0, half, part_sent, 0)
    inputs.finish()
    contexts.finish()
    context_keep.wait()
    context_copy().wait()
    gram_copy().wait()


def widen(factor, context_ref, input_ref, gram_ref, context_out, input_out, gram_out):
    context_out[...] = context_ref[...]
    input_out[...] = input_ref[...].astype(jnp.float32) * factor
    gram_out[...] = gram_ref[...].astype(jnp.float32) * factor


def on_device_fused(activations, ln_gain, w_qkv):
    row_count, feature_count = activations.shape
    heads, triple = w_qkv.shape[1:]
    head_weight = jnp.transpose(w_qkv, (1, 0, 2))
    tokens = row_count * lax.axis_size("mx")
    length, block = lax.axis_size("dp"), feature_count // 2
    gathered = pltpu.VMEM((length, tokens, block), jnp.bfloat16)
    part = pltpu.VMEM((heads // 2, tokens, triple), jnp.bfloat16)
    dma = pltpu.SemaphoreType.DMA
    whole = pl.BlockSpec(memory_space=pltpu.VMEM)
    shapes = ((tokens // 2, 2 * block), (block, block), (2 * block, block // 2))
    results = pl.pallas_call(
        functools.partial(kernel, length, triple // 3),
        out_shape=tuple(jax.ShapeDtypeStruct(shape, jnp.bfloat16) for shape in shapes),
        in_specs=[whole, whole, pl.BlockSpec(memory_space=pl.ANY)],
        out_specs=(whole, whole, whole),
        scratch_shapes=[
            pltpu.VMEM((row_count, feature_count), jnp.bfloat16),
            pltpu.VMEM((2, row_count, 128), jnp.float32),
            pltpu.VMEM((2, row_count, 128), jnp.float32),
            pltpu.VMEM((block, block), jnp.float32),
            pltpu.VMEM((block, block // 2), jnp.bfloat16),
            pltpu.VMEM((tokens, feature_count), jnp.bfloat16),
            pltpu.VMEM((heads, feature_count, triple), jnp.bfloat16),
            part, part, part,
            gathered, gathered, gathered, gathered,
            pltpu.VMEM((block, block), jnp.float32),
            dma((heads,)),
            dma((2, 2)),
            dma((heads // 2,)),
            dma((heads // 2,)),
            dma((2, 2, length, 2)),
            dma((2, 2, length, 2)),
            dma((2, length, 2, 2)),
            dma((2, length, 2)),
            dma((2, length, 2)),
            dma((5,)),
            dma((2,)),
            dma((2,)),
        ],
        compiler_params=pltpu.CompilerParams(
            collective_id=0, has_side_effects=True, vmem_limit_bytes=60 * 1024 * 1024
        ),
        cost_estimate=pl.CostEstimate(
            flops=14_000_000_000, bytes_accessed=24_000_000, transcendentals=2_000_000
        ),
        name="attention_grams",
    )(activations, ln_gain[None, :], head_weight)
    steps = 4
    specs = [pl.BlockSpec((rows // steps, width), lambda i: (i, 0)) for rows, width in shapes]
    kinds = (jnp.bfloat16, jnp.float32, jnp.float32)
    return tuple(
        pl.pallas_call(
            functools.partial(widen, 2.0 / (tokens * length)),
            out_shape=tuple(
                jax.ShapeDtypeStruct(shape, kind) for shape, kind in zip(shapes, kinds)
            ),
            grid=(steps,),
            in_specs=specs,
            out_specs=tuple(specs),
            compiler_params=pltpu.CompilerParams(vmem_limit_bytes=60 * 1024 * 1024),
            name="widen_results",
        )(*results)
    )


def solution(mesh):
    placed = (P(("groups", "dp", "mx"), "my"), P("my"), P("my", "mx", None))
    fused = mesh.shape["mx"] == 2 and mesh.shape["my"] == 2 and mesh.shape["dp"] == 4
    return jax.shard_map(
        on_device_fused if fused else on_device,
        mesh=mesh,
        in_specs=placed,
        out_specs=(
            P(("groups", "dp", "my"), "mx"),
            P(("groups", "mx", "my"), "dp"),
            P(("groups", "mx"), ("dp", "my")),
        ),
        check_vma=False,
    )
```

```python
import functools

import jax
import jax.numpy as jnp
from jax import lax
from jax.experimental import pallas as pl
from jax.experimental.pallas import tpu as pltpu
from jax.sharding import PartitionSpec as P

EPSILON = 1e-06
MESH = pl.DeviceIdType.MESH


def spread_2(block, axis, owner):
    block = jnp.where(lax.axis_index(axis) == owner, block, jnp.zeros_like(block))
    return lax.psum(block, axis)


def layer_norm(inputs):
    average = jnp.mean(inputs, -1, keepdims=True)
    squares = jnp.mean(inputs * inputs, -1, keepdims=True)
    return (inputs - average) * lax.rsqrt(squares - average * average + EPSILON)


def gram_product(left_side, right_side):
    return lax.dot_general(
        left_side, right_side, (((0,), (0,)), ((), ())), preferred_element_type=jnp.float32
    )


def on_device(activations, ln_gain, w_qkv):
    row_count, feature_count = activations.shape
    widened = activations.astype(jnp.float32)
    row_sums, row_squares = lax.psum((jnp.sum(widened, 1), jnp.sum(widened * widened, 1)), "my")
    width = feature_count * lax.axis_size("my")
    average = (row_sums / width)[:, None]
    spread = (row_squares / width)[:, None] - average * average
    normed = ((widened - average) * lax.rsqrt(spread + EPSILON) * ln_gain).astype(jnp.bfloat16)
    image_rows = lax.all_gather(normed, "mx", axis=0, tiled=True)
    local_heads, triple = (w_qkv.shape[1], w_qkv.shape[2])
    head_size = triple // 3
    flat_weight = w_qkv.reshape(feature_count, local_heads * triple)
    own_rows = image_rows.shape[0] // lax.axis_size("my")
    projected = (
        lax.psum_scatter(
            jnp.dot(image_rows, flat_weight, preferred_element_type=jnp.float32).astype(
                jnp.bfloat16
            ),
            "my",
            scatter_dimension=0,
            tiled=True,
        )
        .astype(jnp.float32)
        .reshape(own_rows, local_heads, triple)
    )
    queries = layer_norm(projected[:, :, :head_size]).astype(jnp.bfloat16)
    key_rows = layer_norm(projected[:, :, head_size : 2 * head_size]).astype(jnp.bfloat16)
    value_rows = projected[:, :, 2 * head_size :].astype(jnp.bfloat16)
    all_keys, all_values = (
        lax.all_gather(key_rows, "my", axis=0, tiled=True),
        lax.all_gather(value_rows, "my", axis=0, tiled=True),
    )
    scores = jnp.einsum(
        "qhd,khd->hqk", queries, all_keys, preferred_element_type=jnp.float32
    ) * head_size ** (-0.5)
    powers = jnp.exp(scores)
    totals = jnp.sum(powers, 2)
    weights = powers.astype(jnp.bfloat16)
    mixture = jnp.einsum("hqk,khd->qhd", weights, all_values, preferred_element_type=jnp.float32)
    mixture = mixture / jnp.transpose(totals)[:, :, None]
    context = mixture.astype(jnp.bfloat16).reshape(own_rows, local_heads * head_size)
    full_rows = lax.all_gather(image_rows, "my", axis=1, tiled=True)
    tile_width = full_rows.shape[1] // (lax.axis_size("mx") * lax.axis_size("my"))
    tile_index = lax.axis_index("mx") * lax.axis_size("my") + lax.axis_index("my")
    row_block = lax.dynamic_slice_in_dim(full_rows, tile_index * tile_width, tile_width, 1)
    factor = 2.0 / (full_rows.shape[0] * lax.axis_size("dp"))
    h_input = (
        lax.psum_scatter(
            gram_product(row_block, full_rows).astype(jnp.bfloat16),
            "dp",
            scatter_dimension=1,
            tiled=True,
        ).astype(jnp.float32)
        * factor
    )
    everything = lax.all_gather(context, ("dp", "my"), axis=0, tiled=True)
    block_width = everything.shape[1]
    narrow = block_width * lax.axis_size("mx") // (lax.axis_size("dp") * lax.axis_size("my"))
    flat_index = lax.axis_index("dp") * lax.axis_size("my") + lax.axis_index("my")
    offset = flat_index * narrow
    column_piece = lax.dynamic_slice_in_dim(everything, offset % block_width, narrow, 1)
    columns = spread_2(column_piece, "mx", offset // block_width)
    h_context = gram_product(everything, columns) * factor
    return (context, h_input, h_context)


class Gather:
    def __init__(self, length, place, rows, columns, total, send, receive, share, shared, local):
        self.length, (self.z, self.x, self.c) = length, place
        self.rows, self.columns, self.total = rows, columns, total
        self.send, self.receive = send, receive
        self.share, self.shared, self.local = share, shared, local
        block = 2 * self.x + self.c
        self.owner = block == self.z
        self.relay = (self.x != self.z // 2) & (self.c == self.z % 2)

    def image(self, way, step):
        return self.z - step if way == 0 else self.z + step

    def valid(self, way, step):
        return self.z >= step if way == 0 else self.z + step < self.length

    def tokens(self, part):
        rows = self.rows.shape[1] // 2
        half = self.x if part == 0 else 1 - self.x
        return pl.ds(pl.multiple_of(half * rows, rows), rows)

    def hop(self, way, step, part):
        image = self.image(way, step)
        return pltpu.make_async_remote_copy(
            src_ref=self.rows.at[image, self.tokens(part)],
            dst_ref=self.rows.at[image, self.tokens(part)],
            send_sem=self.send.at[way, step, part],
            recv_sem=self.receive.at[way, step, part],
            device_id={"dp": self.z + 1 if way == 0 else self.z - 1},
            device_id_type=MESH,
        )

    def hops(self, way, step):
        inside = self.z < self.length - 1 if way == 0 else self.z > 0
        return inside & self.valid(way, step)

    def arrival(self, way, step, part):
        image = self.image(way, step)
        return pltpu.make_async_remote_copy(
            src_ref=self.rows.at[image, self.tokens(part)],
            dst_ref=self.rows.at[image, self.tokens(part)],
            send_sem=self.send.at[way, step, part],
            recv_sem=self.receive.at[way, step - 1, part],
            device_id={"dp": self.z - 1 if way == 0 else self.z + 1},
            device_id_type=MESH,
        )

    def sharing(self, source, image, axis, part):
        other = {"my": 1 - self.c} if axis == 0 else {"mx": 1 - self.x}
        return pltpu.make_async_remote_copy(
            src_ref=source.at[image, self.tokens(part)],
            dst_ref=self.columns.at[image, self.tokens(part)],
            send_sem=self.share.at[image, axis, self.part_of(part)],
            recv_sem=self.shared.at[image, self.part_of(part)],
            device_id=other,
            device_id_type=MESH,
        )

    def part_of(self, part):
        return self.x if part == 0 else 1 - self.x

    def own(self, image, part):
        return pltpu.make_async_copy(
            self.rows.at[image, self.tokens(part)],
            self.columns.at[image, self.tokens(part)],
            self.local.at[image, part],
        )

    def spread(self, image, part):
        @pl.when(self.owner)
        def _():
            self.sharing(self.rows, image, 1, part).start()
            self.sharing(self.rows, image, 0, part).start()
            self.own(image, part).start()

    def begin(self, part):
        for way in range(2):

            @pl.when(self.hops(way, 0))
            def _():
                self.hop(way, 0, part).start()

        self.spread(self.z, part)

    def forward(self, step, part):
        for way in range(2):

            @pl.when(self.valid(way, step))
            def _():
                self.arrival(way, step, part).wait_recv()
                if step < self.length - 1:

                    @pl.when(self.hops(way, step))
                    def _():
                        self.hop(way, step, part).start()

                self.spread(self.image(way, step), part)

    def follow(self, image, half):
        rows = self.rows.shape[1] // 2
        tokens = pl.ds(pl.multiple_of(half * rows, rows), rows)
        onward = pltpu.make_async_remote_copy(
            src_ref=self.columns.at[image, tokens],
            dst_ref=self.columns.at[image, tokens],
            send_sem=self.share.at[image, 0, half],
            recv_sem=self.shared.at[image, half],
            device_id={"my": 1 - self.c},
            device_id_type=MESH,
        )

        @pl.when(jnp.logical_not(self.owner))
        def _():
            onward.wait_recv()

        @pl.when(self.relay)
        def _():
            onward.start()

    def take(self, image, first):
        for order in range(2):

            @pl.when(self.owner)
            def _():
                self.own(image, order).wait()

            half = self.z // 2 if order == 0 else 1 - self.z // 2
            self.follow(image, half)

        def piece(index, carry):
            part = pl.ds(pl.multiple_of(index * 256, 256), 256)
            term = lax.dot_general(
                self.rows[image, :, part],
                self.columns[image],
                (((0,), (0,)), ((), ())),
                preferred_element_type=jnp.float32,
            )
            if first:
                self.total[part, :] = term
            else:
                self.total[part, :] += term
            return carry

        lax.fori_loop(0, self.total.shape[0] // 256, piece, 0)

    def consume(self, step):
        if step == 0:
            self.take(self.z, True)
            return
        for way in range(2):

            @pl.when(self.valid(way, step))
            def _():
                self.take(self.image(way, step), False)

    def finish(self):
        for way in range(2):
            for step in range(self.length - 1):

                @pl.when(self.hops(way, step))
                def _():
                    for part in range(2):
                        self.hop(way, step, part).wait_send()

        def one(image, carry):
            for part in range(2):

                @pl.when(self.owner)
                def _():
                    self.sharing(self.rows, image, 1, part).wait_send()
                    self.sharing(self.rows, image, 0, part).wait_send()

                @pl.when(self.relay)
                def _():
                    self.sharing(self.columns, image, 0, part).wait_send()

            return carry

        lax.fori_loop(0, self.length, one, 0)


def kernel(
    length, head_size,
    activation_ref, gain_ref, weight_ref, context_ref, input_ref, gram_ref,
    normed_ref, sums, other_sums, input_total, leaving_gram, image_ref, weights, leaving, kept, arrived,
    input_rows, input_columns, context_rows, context_columns, total,
    weight_sem, plane_sem, part_send, part_receive,
    line_send, line_receive, share_send, share_receive, local_sem, swap_sem, side_sem, sum_sem,
):
    z, x, c = lax.axis_index("dp"), lax.axis_index("mx"), lax.axis_index("my")
    heads, _, triple = weights.shape
    half = heads // 2
    tokens, block = input_rows.shape[1:]

    def weight_copy(position):
        head = lax.rem(position + (1 - c) * half, heads)
        return pltpu.make_async_copy(
            weight_ref.at[head], weights.at[position], weight_sem.at[position]
        )

    def start_weight(position, carry):
        weight_copy(position).start()
        return carry

    lax.fori_loop(0, heads, start_weight, 0)

    features = activation_ref.shape[1]
    tile = 64

    def tile_rows(index):
        return pl.ds(pl.multiple_of(index * tile, tile), tile)

    def add_up(index, carry):
        rows = tile_rows(index)
        values = activation_ref[rows, :].astype(jnp.float32)
        lanes = (tile, sums.shape[2])
        sums[0, rows] = jnp.broadcast_to(jnp.sum(values, 1, keepdims=True), lanes)
        sums[1, rows] = jnp.broadcast_to(jnp.sum(values * values, 1, keepdims=True), lanes)
        return carry

    lax.fori_loop(0, activation_ref.shape[0] // tile, add_up, 0)

    barrier = pltpu.get_barrier_semaphore()
    pl.semaphore_signal(barrier, inc=1, device_id={"my": 1 - c}, device_id_type=MESH)
    pl.semaphore_signal(barrier, inc=1, device_id={"mx": 1 - x}, device_id_type=MESH)

    @pl.when(z > 0)
    def _():
        pl.semaphore_signal(barrier, inc=1, device_id={"dp": z - 1}, device_id_type=MESH)

    @pl.when(z < length - 1)
    def _():
        pl.semaphore_signal(barrier, inc=1, device_id={"dp": z + 1}, device_id_type=MESH)

    edges = jnp.where(z > 0, 1, 0) + jnp.where(z < length - 1, 1, 0)
    pl.semaphore_wait(barrier, 2 + edges)

    def sum_copy():
        return pltpu.make_async_remote_copy(
            src_ref=sums,
            dst_ref=other_sums,
            send_sem=sum_sem.at[0],
            recv_sem=sum_sem.at[1],
            device_id={"my": 1 - c},
            device_id_type=MESH,
        )

    sum_copy().start()
    sum_copy().wait()

    def normalise(index, carry):
        rows = tile_rows(index)
        width = features * 2
        average = (sums[0, rows, 0:1] + other_sums[0, rows, 0:1]) / width
        squares = (sums[1, rows, 0:1] + other_sums[1, rows, 0:1]) / width
        values = activation_ref[rows, :].astype(jnp.float32)
        scale = lax.rsqrt(squares - average * average + EPSILON)
        normed_ref[rows, :] = ((values - average) * scale * gain_ref[...][None, :]).astype(jnp.bfloat16)
        return carry

    lax.fori_loop(0, activation_ref.shape[0] // tile, normalise, 0)

    inputs = Gather(
        length, (z, x, c), input_rows, input_columns, input_total,
        line_send.at[0], line_receive.at[0], share_send.at[0], share_receive.at[0], local_sem.at[0],
    )
    contexts = Gather(
        length, (z, x, c), context_rows, context_columns, total,
        line_send.at[1], line_receive.at[1], share_send.at[1], share_receive.at[1], local_sem.at[1],
    )

    side = tokens // 2
    own_side = pl.ds(pl.multiple_of(x * side, side), side)
    far_side = pl.ds(pl.multiple_of((1 - x) * side, side), side)

    def side_copy():
        return pltpu.make_async_remote_copy(
            src_ref=normed_ref,
            dst_ref=image_ref.at[own_side],
            send_sem=side_sem.at[0],
            recv_sem=side_sem.at[1],
            device_id={"mx": 1 - x},
            device_id_type=MESH,
        )

    def plane_copy(part):
        away = pl.ds(pl.multiple_of((1 - c) * block, block), block)
        source = normed_ref.at[:, away] if part == 0 else image_ref.at[far_side, away]
        return pltpu.make_async_remote_copy(
            src_ref=source,
            dst_ref=input_rows.at[z, own_side if part == 0 else far_side],
            send_sem=plane_sem.at[0, part],
            recv_sem=plane_sem.at[1, part],
            device_id={"my": 1 - c},
            device_id_type=MESH,
        )

    def start_inputs(part):
        mine = pl.ds(pl.multiple_of(c * block, block), block)

        @pl.when(c == x)
        def _():
            if part == 1:
                side_copy().wait_recv()
            plane_copy(part).start()
            if part == 0:
                input_rows[z, own_side] = normed_ref[:, mine]
            else:
                input_rows[z, far_side] = image_ref[far_side, mine]

        @pl.when(c != x)
        def _():
            plane_copy(part).wait_recv()

        inputs.begin(part)

    @pl.when(c != x)
    def _():
        side_copy().start()

    start_inputs(0)

    def part_copy(index):
        return pltpu.make_async_remote_copy(
            src_ref=leaving.at[index],
            dst_ref=arrived.at[index],
            send_sem=part_send.at[index],
            recv_sem=part_receive.at[index],
            device_id={"my": 1 - c},
            device_id_type=MESH,
        )

    def product(rows, position):
        return jnp.dot(rows, weights[position], preferred_element_type=jnp.float32).astype(
            jnp.bfloat16
        )

    def away_near(index, carry):
        weight_copy(index).wait()
        leaving[index, own_side] = product(normed_ref[...], index)
        return carry

    def here_near(index, carry):
        weight_copy(half + index).wait()
        kept[index, own_side] = product(normed_ref[...], half + index)
        return carry

    def away_far(index, carry):
        leaving[index, far_side] = product(image_ref[far_side], index)
        part_copy(index).start()
        return carry

    def here_far(index, carry):
        kept[index, far_side] = product(image_ref[far_side], half + index)
        return carry

    lax.fori_loop(0, half, away_near, 0)

    @pl.when(c == x)
    def _():
        side_copy().start()

    lax.fori_loop(0, half, here_near, 0)
    start_inputs(1)

    @pl.when(c != x)
    def _():
        side_copy().wait_recv()

    lax.fori_loop(0, half, away_far, 0)
    inputs.forward(1, 0)
    lax.fori_loop(0, half, here_far, 0)
    inputs.forward(1, 1)

    def norm(values):
        average = jnp.mean(values, -1, keepdims=True)
        squares = jnp.mean(values * values, -1, keepdims=True)
        return ((values - average) * lax.rsqrt(squares - average * average + EPSILON)).astype(
            jnp.bfloat16
        )

    def attend(part, index, carry):
        rows = own_side if part == 0 else far_side
        if part == 0:
            part_copy(index).wait_recv()

        def projected(tokens, first, last):
            return kept[index, tokens, first:last].astype(jnp.float32) + arrived[
                index, tokens, first:last
            ].astype(jnp.float32)

        every = slice(None)
        queries = norm(projected(rows, 0, head_size))
        keys = norm(projected(every, head_size, 2 * head_size))
        values = projected(every, 2 * head_size, 3 * head_size).astype(jnp.bfloat16)
        scores = lax.dot_general(
            queries, keys, (((1,), (1,)), ((), ())), preferred_element_type=jnp.float32
        ) * head_size ** (-0.5)
        powers = jnp.exp(scores)
        totals = jnp.sum(powers, 1, keepdims=True)
        mixture = jnp.dot(
            powers.astype(jnp.bfloat16), values, preferred_element_type=jnp.float32
        )
        place = pl.ds(pl.multiple_of(index * head_size, head_size), head_size)
        context_rows[z, rows, place] = (mixture / totals).astype(jnp.bfloat16)
        return carry

    lax.fori_loop(0, half, functools.partial(attend, 0), 0)
    contexts.begin(0)
    inputs.forward(2, 0)
    lax.fori_loop(0, half, functools.partial(attend, 1), 0)
    contexts.begin(1)

    own_tokens = tokens // 2
    place = pl.ds(pl.multiple_of(c * block, block), block)

    def context_copy():
        away = pl.ds(pl.multiple_of((1 - c) * own_tokens, own_tokens), own_tokens)
        return pltpu.make_async_remote_copy(
            src_ref=context_rows.at[z, away],
            dst_ref=context_ref.at[:, place],
            send_sem=swap_sem.at[0],
            recv_sem=swap_sem.at[1],
            device_id={"my": 1 - c},
            device_id_type=MESH,
        )

    context_copy().start()
    here = pl.ds(pl.multiple_of(c * own_tokens, own_tokens), own_tokens)
    context_keep = pltpu.make_async_copy(
        context_rows.at[z, here], context_ref.at[:, place], swap_sem.at[2]
    )
    context_keep.start()

    inputs.consume(0)
    inputs.forward(2, 1)
    inputs.consume(1)
    contexts.forward(1, 0)
    contexts.forward(1, 1)
    contexts.consume(0)
    for step in range(3, length):
        inputs.forward(step, 0)
        inputs.forward(step, 1)
        inputs.consume(step - 1)
        contexts.forward(step - 1, 0)
        contexts.forward(step - 1, 1)
        contexts.consume(step - 2)
    inputs.consume(length - 1)
    input_ref[...] = input_total[...].astype(jnp.bfloat16)
    contexts.consume(length - 2)
    contexts.forward(length - 1, 0)
    contexts.forward(length - 1, 1)
    contexts.consume(length - 1)

    narrow = block // 2
    rows = pl.ds(pl.multiple_of(c * block, block), block)
    leaving_gram[...] = total[
        :, pl.ds(pl.multiple_of((1 - c) * narrow, narrow), narrow)
    ].astype(jnp.bfloat16)

    def gram_copy():
        return pltpu.make_async_remote_copy(
            src_ref=leaving_gram,
            dst_ref=gram_ref.at[rows],
            send_sem=swap_sem.at[3],
            recv_sem=swap_sem.at[4],
            device_id={"my": 1 - c},
            device_id_type=MESH,
        )

    gram_copy().start()
    gram_ref[rows, :] = total[
        :, pl.ds(pl.multiple_of(c * narrow, narrow), narrow)
    ].astype(jnp.bfloat16)

    @pl.when(c == x)
    def _():
        plane_copy(0).wait_send()
        plane_copy(1).wait_send()

    side_copy().wait_send()

    def part_sent(index, carry):
        part_copy(index).wait_send()
        return carry

    lax.fori_loop(0, half, part_sent, 0)
    inputs.finish()
    contexts.finish()
    context_keep.wait()
    context_copy().wait()
    gram_copy().wait()


def widen(factor, context_ref, input_ref, gram_ref, context_out, input_out, gram_out):
    context_out[...] = context_ref[...]
    input_out[...] = input_ref[...].astype(jnp.float32) * factor
    gram_out[...] = gram_ref[...].astype(jnp.float32) * factor


def on_device_fused(activations, ln_gain, w_qkv):
    row_count, feature_count = activations.shape
    heads, triple = w_qkv.shape[1:]
    head_weight = jnp.transpose(w_qkv, (1, 0, 2))
    tokens = row_count * lax.axis_size("mx")
    length, block = lax.axis_size("dp"), feature_count // 2
    gathered = pltpu.VMEM((length, tokens, block), jnp.bfloat16)
    part = pltpu.VMEM((heads // 2, tokens, triple), jnp.bfloat16)
    dma = pltpu.SemaphoreType.DMA
    whole = pl.BlockSpec(memory_space=pltpu.VMEM)
    shapes = ((tokens // 2, 2 * block), (block, block), (2 * block, block // 2))
    results = pl.pallas_call(
        functools.partial(kernel, length, triple // 3),
        out_shape=tuple(jax.ShapeDtypeStruct(shape, jnp.bfloat16) for shape in shapes),
        in_specs=[whole, whole, pl.BlockSpec(memory_space=pl.ANY)],
        out_specs=(whole, whole, whole),
        scratch_shapes=[
            pltpu.VMEM((row_count, feature_count), jnp.bfloat16),
            pltpu.VMEM((2, row_count, 128), jnp.float32),
            pltpu.VMEM((2, row_count, 128), jnp.float32),
            pltpu.VMEM((block, block), jnp.float32),
            pltpu.VMEM((block, block // 2), jnp.bfloat16),
            pltpu.VMEM((tokens, feature_count), jnp.bfloat16),
            pltpu.VMEM((heads, feature_count, triple), jnp.bfloat16),
            part, part, part,
            gathered, gathered, gathered, gathered,
            pltpu.VMEM((block, block), jnp.float32),
            dma((heads,)),
            dma((2, 2)),
            dma((heads // 2,)),
            dma((heads // 2,)),
            dma((2, 2, length, 2)),
            dma((2, 2, length, 2)),
            dma((2, length, 2, 2)),
            dma((2, length, 2)),
            dma((2, length, 2)),
            dma((5,)),
            dma((2,)),
            dma((2,)),
        ],
        compiler_params=pltpu.CompilerParams(
            collective_id=0, has_side_effects=True, vmem_limit_bytes=60 * 1024 * 1024
        ),
        cost_estimate=pl.CostEstimate(
            flops=14_000_000_000, bytes_accessed=24_000_000, transcendentals=2_000_000
        ),
        name="attention_grams",
    )(activations, ln_gain, head_weight)
    steps = 4
    specs = [pl.BlockSpec((rows // steps, width), lambda i: (i, 0)) for rows, width in shapes]
    kinds = (jnp.bfloat16, jnp.float32, jnp.float32)
    return tuple(
        pl.pallas_call(
            functools.partial(widen, 2.0 / (tokens * length)),
            out_shape=tuple(
                jax.ShapeDtypeStruct(shape, kind) for shape, kind in zip(shapes, kinds)
            ),
            grid=(steps,),
            in_specs=specs,
            out_specs=tuple(specs),
            compiler_params=pltpu.CompilerParams(vmem_limit_bytes=60 * 1024 * 1024),
            name="widen_results",
        )(*results)
    )


def solution(mesh):
    placed = (P(("groups", "dp", "mx"), "my"), P("my"), P("my", "mx", None))
    fused = mesh.shape["mx"] == 2 and mesh.shape["my"] == 2 and mesh.shape["dp"] == 4
    return jax.shard_map(
        on_device_fused if fused else on_device,
        mesh=mesh,
        in_specs=placed,
        out_specs=(
            P(("groups", "dp", "my"), "mx"),
            P(("groups", "mx", "my"), "dp"),
            P(("groups", "mx"), ("dp", "my")),
        ),
        check_vma=False,
    )
```
